32 devices in a mesh: dp: 16 (over z, y, core), tensor: 2 (over x).
Axes of the slice: x: 2, y: 2, z: 4, core: 2. Of those that a mesh axis runs over, the one named last changes fastest.
Arguments:
- tokens: bfloat16 [32768, 1024], P(('dp', 'tensor')), may hold values from -6 to 6
- doc_lengths: int32 [32, 4], P('dp'), may hold values from 1 to 800, 1024 in all within a row
- ln1_gain: bfloat16 [1024], replicated, may hold values from 0.099609375 to 1.8984375
- ln1_bias: bfloat16 [1024], replicated, may hold values from -1.5 to 1.5
- w_query: bfloat16 [1024, 1024], P('dp', 'tensor'), may hold values from -0.1875 to 0.1875
- b_query: bfloat16 [1024], P('tensor'), may hold values from -2.5 to 2.5
- w_key: bfloat16 [1024, 1024], P('dp', 'tensor'), may hold values from -0.1875 to 0.1875
- w_value: bfloat16 [1024, 1024], P('dp', 'tensor'), may hold values from -0.1875 to 0.1875
- b_value: bfloat16 [1024], P('tensor'), may hold values from -2.5 to 2.5
- w_dense: bfloat16 [1024, 1024], P('tensor', 'dp'), may hold values from -0.5 to 0.5
- b_dense: bfloat16 [1024], replicated, may hold values from -2.5 to 2.5
- ln2_gain: bfloat16 [1024], replicated, may hold values from 0.099609375 to 1.8984375
- ln2_bias: bfloat16 [1024], replicated, may hold values from -1.5 to 1.5
- w_up: bfloat16 [1024, 4096], P('dp', 'tensor'), may hold values from -0.1875 to 0.1875
- b_up: bfloat16 [4096], P('tensor'), may hold values from -2.5 to 2.5
- w_down: bfloat16 [4096, 1024], P('tensor', 'dp'), may hold values from -0.125 to 0.125
- b_down: bfloat16 [1024], replicated, may hold values from -2.5 to 2.5
- out_grad: bfloat16 [32768, 1024], P(('dp', 'tensor')), may hold values from -6 to 6
Outputs:
- mixed: bfloat16 [32768, 1024], P(('dp', 'tensor'))
- tokens_grad: bfloat16 [32768, 1024], P(('dp', 'tensor'))
- ln1_gain_grad: float32 [1024], replicated
- ln1_bias_grad: float32 [1024], replicated
- w_query_grad: float32 [1024, 1024], P('dp', 'tensor')
- b_query_grad: float32 [1024], P('tensor')
- w_key_grad: float32 [1024, 1024], P('dp', 'tensor')
- w_value_grad: float32 [1024, 1024], P('dp', 'tensor')
- b_value_grad: float32 [1024], P('tensor')
- w_dense_grad: float32 [1024, 1024], P('tensor', 'dp')
- b_dense_grad: float32 [1024], replicated
- ln2_gain_grad: float32 [1024], replicated
- ln2_bias_grad: float32 [1024], replicated
- w_up_grad: float32 [1024, 4096], P('dp', 'tensor')
- b_up_grad: float32 [4096], P('tensor')
- w_down_grad: float32 [4096, 1024], P('tensor', 'dp')
- b_down_grad: float32 [1024], replicated
The draws below stay inside these ranges and needn't reach their ends.
Inputs may be any that keep to these rules, and one draw needn't show every extreme that they name: `doc_lengths`: each row holds the lengths of the 4 documents of one sequence in order; they sum to 1024, and each row's longest is exactly 800.
All inputs are finite; a program needn't handle non-finite values.
Results may differ from the reference program's by a relative error of at most 0.018.
Values may be sent and summed in bfloat16 or wider, within the bound.
A program may use at most 192 MiB of HBM per device.

```python
import math
import jax
import jax.numpy as jnp
import numpy as np
from jax import lax

D = 1024
HEADS = 16
HDIM = 64
FF = 4096
SEQ_LEN = 1024
DOCS = 4
LONGEST = 800
NSEQ = 32
TOKENS = 32768


def level_of(rng, shape, cuts, least, top_value):
    def one(axis_at, shards_of):
        steps = jax.random.uniform(jax.random.fold_in(jax.random.fold_in(rng, 6), axis_at), (shards_of,), jnp.float32, least / len(cuts), top_value / len(cuts))
        return jnp.repeat(jnp.exp(steps), shape[axis_at] // shards_of).reshape((-1,) + (1,) * (len(shape) - axis_at - 1))

    loudness = one(*cuts[0])
    for cut in cuts[1:]:
        loudness = loudness * one(*cut)
    return loudness


def profile(number_of, total, most, skew):
    portions = [(1 << 20) // math.isqrt(grade ** skew) + 1 for grade in range(2, number_of + 1)]
    rest, counts = total - most - (number_of - 1), [1] * (number_of - 1)
    while rest > 0:
        candidates = [i for i in range(number_of - 1) if counts[i] < most]
        pool, left = sum([portions[i] for i in candidates]), rest
        for i in candidates:
            addition = min(most - counts[i], max(1, left * portions[i] // pool), rest)
            counts[i] = counts[i] + addition
            rest = rest - addition
    return np.array([most] + counts)


def ragged_sizes(own_key, count, total, bound, lean):
    if count == 2:
        one = jax.random.randint(own_key, (), max(1, total - bound), min(bound, total - 1) + 1)
        return jnp.stack([one, total - one])
    sizes = jnp.asarray(profile(count, total, bound, lean), jnp.int32)
    couples = (count - 1) // 2
    source_of, taker = sizes[1:1 + 2 * couples:2], sizes[2:2 + 2 * couples:2]
    margin = jnp.minimum(source_of - 1, bound - taker)
    moved = jax.random.randint(jax.random.fold_in(own_key, 1), (couples,), 0, 1 << 20) % (margin + 1)
    sizes = sizes.at[1:1 + 2 * couples:2].set(source_of - moved).at[2:2 + 2 * couples:2].set(taker + moved)
    return sizes[jax.random.permutation(jax.random.fold_in(own_key, 2), count)]


def scatter_about(stream_key, shape, scale, most, pieces=(), kind=jnp.bfloat16):
    drawn = scale * jax.random.normal(stream_key, shape, jnp.float32)
    if pieces:
        drawn = drawn * level_of(stream_key, shape, pieces, -0.22, 0.18)
    return jnp.clip(drawn, -most, most).astype(kind)


def setup_inputs(seed: int = 0) -> dict:
    arg_keys = jax.random.split(jax.random.key(seed), 19)
    tokens = scatter_about(arg_keys[0], (TOKENS, D), 1.0, 6.0, ((0, 32),))
    doc_lengths = jax.vmap(lambda own: ragged_sizes(own, DOCS, SEQ_LEN, LONGEST, 2))(jax.random.split(arg_keys[1], NSEQ)).reshape((NSEQ, DOCS)).astype(jnp.int32)
    ln1_gain = jnp.clip(1.0 + 0.18 * jax.random.normal(arg_keys[2], (D,), jnp.float32), 0.099609375, 1.8984375).astype(jnp.bfloat16)
    ln1_bias = scatter_about(arg_keys[3], (D,), 0.3, 1.5)
    w_query = scatter_about(arg_keys[4], (D, D), D ** -0.5, 0.1875, ((0, 16), (1, 2)))
    b_query = scatter_about(arg_keys[5], (D,), 0.5, 2.5, ((0, 2),))
    w_key = scatter_about(arg_keys[6], (D, D), D ** -0.5, 0.1875, ((0, 16), (1, 2)))
    w_value = scatter_about(arg_keys[7], (D, D), D ** -0.5, 0.1875, ((0, 16), (1, 2)))
    b_value = scatter_about(arg_keys[8], (D,), 0.5, 2.5, ((0, 2),))
    w_dense = scatter_about(arg_keys[9], (D, D), (D // 8) ** -0.5, 0.5, ((0, 2), (1, 16)))
    b_dense = scatter_about(arg_keys[10], (D,), 0.5, 2.5)
    ln2_gain = jnp.clip(1.0 + 0.18 * jax.random.normal(arg_keys[11], (D,), jnp.float32), 0.099609375, 1.8984375).astype(jnp.bfloat16)
    ln2_bias = scatter_about(arg_keys[12], (D,), 0.3, 1.5)
    w_up = scatter_about(arg_keys[13], (D, FF), D ** -0.5, 0.1875, ((0, 16), (1, 2)))
    b_up = scatter_about(arg_keys[14], (FF,), 0.5, 2.5, ((0, 2),))
    w_down = scatter_about(arg_keys[15], (FF, D), (FF // 2) ** -0.5, 0.125, ((0, 2), (1, 16)))
    b_down = scatter_about(arg_keys[16], (D,), 0.5, 2.5)
    out_grad = scatter_about(arg_keys[17], (TOKENS, D), 1.0, 6.0, ((0, 32),))
    return {"tokens": tokens, "doc_lengths": doc_lengths, "ln1_gain": ln1_gain, "ln1_bias": ln1_bias, "w_query": w_query, "b_query": b_query, "w_key": w_key, "w_value": w_value, "b_value": b_value, "w_dense": w_dense, "b_dense": b_dense, "ln2_gain": ln2_gain, "ln2_bias": ln2_bias, "w_up": w_up, "b_up": b_up, "w_down": w_down, "b_down": b_down, "out_grad": out_grad}


@jax.custom_vjp
def low(v):
    return lax.optimization_barrier(v.astype(jnp.bfloat16)).astype(jnp.float32)

@jax.custom_vjp
def low_back(v):
    return v

def low_keep(v):
    return (low(v), None)

def low_pass(kept, grad):
    return (grad,)

def back_keep(v):
    return (v, None)

def back_low(kept, grad):
    return (low(grad),)
low.defvjp(low_keep, low_pass)
low_back.defvjp(back_keep, back_low)
epsilon = 1e-05
highest = lax.Precision.HIGHEST

def rounded_both(field):
    return low(low_back(field))

def layer_norm(field, norm_gain, norm_shift):
    average = lax.optimization_barrier(jnp.mean(field, -1, keepdims=True))
    centred = field - average
    factor = lax.rsqrt(lax.optimization_barrier(jnp.mean(centred * centred, -1, keepdims=True)) + epsilon)
    return centred * factor * norm_gain + norm_shift

def attend_sequence(members):
    query, keys_all, values_all, segment_ids = members
    length = query.shape[0]
    heads = query.shape[1]
    slopes = 2.0 ** (-8.0 * (jnp.arange(heads, dtype=jnp.float32) + 1.0) / heads)
    places = jnp.arange(length, dtype=jnp.int32)
    distance = (places[None, :] - places[:, None]).astype(jnp.float32)
    allowed = (places[None, :] <= places[:, None]) & (segment_ids[None, :] == segment_ids[:, None])
    scores = jnp.einsum('qhd,khd->hqk', query, keys_all, precision=highest) * query.shape[2] ** (-0.5)
    scores = low_back(scores + slopes[:, None, None] * distance[None])
    scores = jnp.where(allowed[None], scores, -1e+30)
    attn_probs = low(jax.nn.softmax(scores, axis=-1))
    return jnp.einsum('hqk,khd->qhd', attn_probs, values_all, precision=highest)

def forward(field, segment_ids, norm1_gain, norm1_shift, w_query, b_query, w_key, w_value, b_value, w_dense, b_dense, norm2_gain, norm2_shift, w_up, b_up, w_down, b_down):
    normed_one = low(layer_norm(field, norm1_gain, norm1_shift))
    query = rounded_both(jnp.dot(normed_one, w_query, precision=highest) + b_query)
    keys_all = rounded_both(jnp.dot(normed_one, w_key, precision=highest))
    values_all = rounded_both(jnp.dot(normed_one, w_value, precision=highest) + b_value)
    split_shape = (NSEQ, SEQ_LEN, HEADS, HDIM)
    context = lax.map(jax.checkpoint(attend_sequence), (query.reshape(split_shape), keys_all.reshape(split_shape), values_all.reshape(split_shape), segment_ids))
    context = rounded_both(context.reshape(TOKENS, D))
    hidden_one = field + low_back(jnp.dot(context, w_dense, precision=highest)) + b_dense
    normed_two = low(layer_norm(hidden_one, norm2_gain, norm2_shift))
    up_field = low_back(jnp.dot(normed_two, w_up, precision=highest) + b_up)
    activated = low(jax.nn.gelu(up_field, approximate=True))
    return hidden_one + low_back(jnp.dot(activated, w_down, precision=highest)) + b_down

def reference(tokens, doc_lengths, ln1_gain, ln1_bias, w_query, b_query, w_key, w_value, b_value, w_dense, b_dense, ln2_gain, ln2_bias, w_up, b_up, w_down, b_down, out_grad):
    doc_ends = jnp.cumsum(doc_lengths, axis=1).astype(jnp.int32)
    places = jnp.arange(SEQ_LEN, dtype=jnp.int32)
    segment_ids = lax.optimization_barrier(jnp.sum((places[None, :, None] >= doc_ends[:, None, :]).astype(jnp.int32), axis=2))
    params = [member.astype(jnp.float32) for member in (ln1_gain, ln1_bias, w_query, b_query, w_key, w_value, b_value, w_dense, b_dense, ln2_gain, ln2_bias, w_up, b_up, w_down, b_down)]

    def layer(field, *weights):
        return forward(field, segment_ids, *weights)
    mixed, pull = jax.vjp(layer, tokens.astype(jnp.float32), *params)
    grads = pull(out_grad.astype(jnp.float32))
    return (mixed.astype(jnp.bfloat16), grads[0].astype(jnp.bfloat16), grads[1], grads[2], grads[3], grads[4], grads[5], grads[6], grads[7], grads[8], grads[9], grads[10], grads[11], grads[12], grads[13], grads[14], grads[15])
```

```python
import jax
import jax.numpy as jnp
from jax import lax
from jax.experimental import pallas as pl
from jax.experimental.pallas import tpu as pltpu
from jax.sharding import PartitionSpec as P

HEADS = 16
HDIM = 64
SEQ_LEN = 1024
SPAN = 256
LANES = 128
FAR = -1e30

epsilon = 1e-05
f32 = jnp.float32
bf16 = jnp.bfloat16


def normalize(field, norm_gain, norm_shift):
    average = jnp.mean(field, -1, keepdims=True)
    centred = field - average
    factor = lax.rsqrt(jnp.mean(centred * centred, -1, keepdims=True) + epsilon)
    normed = centred * factor
    return (normed * norm_gain + norm_shift, normed, factor)


def norm_back(upstream, normed, factor, norm_gain):
    scaled = upstream * norm_gain
    return factor * (
        scaled
        - jnp.mean(scaled, -1, keepdims=True)
        - normed * jnp.mean(scaled * normed, -1, keepdims=True)
    )


def gelu_tanh(field):
    return jax.nn.gelu(field, approximate=True)


def dot(a, b):
    return jnp.dot(a, b, preferred_element_type=f32)


def dot_nt(a, b):
    return lax.dot_general(a, b, (((1,), (1,)), ((), ())), preferred_element_type=f32)


def dot_tn(a, b):
    return lax.dot_general(a, b, (((0,), (0,)), ((), ())), preferred_element_type=f32)


def split_three(field):
    one = field.astype(bf16)
    rest = field - one.astype(f32)
    two = rest.astype(bf16)
    three = (rest - two.astype(f32)).astype(bf16)
    return one.astype(f32), two.astype(f32), three.astype(f32)


def place_columns(doc_lengths, slopes):
    seq_count, docs = doc_lengths.shape
    doc_ends = jnp.cumsum(doc_lengths, axis=1)
    places = jnp.arange(SEQ_LEN, dtype=jnp.int32)
    segment_ids = jnp.sum((places[None, :, None] >= doc_ends[:, None, :]).astype(jnp.int32), axis=2)
    low = (places % 128).astype(f32)
    high = (places - places % 128).astype(f32)
    pairs = jnp.broadcast_to(
        jnp.stack([high, low, high, low], -1)[None], (seq_count, SEQ_LEN, 4)
    )
    none = jnp.zeros((seq_count, SEQ_LEN, 4), f32)
    same = (segment_ids[:, :, None] == jnp.arange(docs)[None, None, :]).astype(f32)
    ones = jnp.ones((seq_count, SEQ_LEN, 3), f32)
    rest = jnp.zeros((seq_count, SEQ_LEN, HDIM - 11 - docs), f32)
    query_half = jnp.concatenate([none, pairs, 0.0 * ones, FAR * (1.0 - same), rest], -1)
    key_half = jnp.concatenate([pairs, none, ones, same, rest], -1)
    query_base = jnp.concatenate([query_half, query_half], -1).astype(bf16)
    key_base = jnp.concatenate([key_half, key_half], -1).astype(bf16)
    first = slopes.astype(bf16).astype(f32)
    second = (slopes - first).astype(bf16).astype(f32)
    four = jnp.stack([first, first, second, second], -1)
    heads = slopes.shape[0]
    blank = jnp.zeros((heads, 4), f32)
    tail = jnp.zeros((heads, HDIM - 8), f32)
    query_line = jnp.concatenate([four, blank, tail], -1)
    key_line = jnp.concatenate([blank, -four, tail], -1)
    lines = jnp.stack([query_line, key_line], 1)
    lines = jnp.concatenate([lines, lines], -1)
    lines = jnp.concatenate([lines, jnp.zeros((heads, 6, LANES), f32)], 1)
    return query_base, key_base, lines.astype(bf16)


def lane_of(rows):
    return lax.broadcasted_iota(jnp.int32, (rows, LANES), 1)


def forward_kernel(qkv_ref, qbase_ref, kbase_ref, lines_ref, out_ref, total_ref):
    upper = lane_of(SEQ_LEN) >= HDIM
    upper_rows = lane_of(SPAN) >= HDIM
    query = (qkv_ref[:, :LANES].astype(f32) * (HDIM**-0.5)).astype(bf16)
    keys = qkv_ref[:, LANES : 2 * LANES]
    values = qkv_ref[:, 2 * LANES :]
    keep = lax.broadcasted_iota(jnp.int32, (SPAN, SPAN), 1) <= lax.broadcasted_iota(
        jnp.int32, (SPAN, SPAN), 0
    )
    found = []
    for head in range(2):
        mine = upper if head else jnp.logical_not(upper)
        query_full = jnp.where(mine, query, qbase_ref[0] + lines_ref[head, 0:1, :])
        keys_full = jnp.where(mine, keys, kbase_ref[0] + lines_ref[head, 1:2, :])
        per_head = []
        for start in range(0, SEQ_LEN, SPAN):
            rows = query_full[start : start + SPAN]
            near = jnp.where(keep, dot_nt(rows, keys_full[start : start + SPAN]), FAR)
            row_max = jnp.max(near, -1, keepdims=True)
            if start:
                past = dot_nt(rows, keys_full[:start])
                row_max = jnp.maximum(row_max, jnp.max(past, -1, keepdims=True))
            near = jnp.exp(near - row_max)
            row_sum = jnp.sum(near, -1, keepdims=True)
            mixed = dot(near.astype(bf16), values[start : start + SPAN])
            if start:
                past = jnp.exp(past - row_max)
                row_sum = row_sum + jnp.sum(past, -1, keepdims=True)
                mixed = mixed + dot(past.astype(bf16), values[:start])
            per_head.append((mixed / row_sum, row_max + jnp.log(row_sum)))
        found.append(per_head)
    for index, start in enumerate(range(0, SEQ_LEN, SPAN)):
        lower_out, lower_total = found[0][index]
        upper_out, upper_total = found[1][index]
        out_ref[start : start + SPAN, :] = jnp.where(upper_rows, upper_out, lower_out).astype(bf16)
        total_ref[start : start + SPAN, :] = jnp.where(upper_rows, upper_total, lower_total)


def backward_kernel(
    qkv_ref, qbase_ref, kbase_ref, lines_ref, out_ref, total_ref, grad_ref, back_ref, hold_ref
):
    lane = lane_of(SEQ_LEN)
    upper = lane >= HDIM
    column = lane % HDIM
    upper_rows = lane_of(SPAN) >= HDIM
    query = (qkv_ref[:, :LANES].astype(f32) * (HDIM**-0.5)).astype(bf16)
    keys = qkv_ref[:, LANES : 2 * LANES]
    values = qkv_ref[:, 2 * LANES :]
    grads = grad_ref[...]
    keep = lax.broadcasted_iota(jnp.int32, (SPAN, SPAN), 0) <= lax.broadcasted_iota(
        jnp.int32, (SPAN, SPAN), 1
    )
    meets = grads.astype(f32) * out_ref[...].astype(f32)
    three_ones = jnp.where(column < 3, 1.0, 0.0).astype(bf16)
    for head in range(2):
        mine = upper if head else jnp.logical_not(upper)
        total = total_ref[:, HDIM : HDIM + 1] if head else total_ref[:, 0:1]
        one, two, three = split_three(-total)
        extra = jnp.where(
            column == 8, one, jnp.where(column == 9, two, jnp.where(column == 10, three, 0.0))
        ).astype(bf16)
        query_full = jnp.where(mine, query, qbase_ref[0] + lines_ref[head, 0:1, :] + extra)
        keys_full = jnp.where(mine, keys, kbase_ref[0] + lines_ref[head, 1:2, :])
        delta = jnp.sum(jnp.where(mine, meets, 0.0), -1, keepdims=True)
        one, two, three = split_three(-delta)
        extra = jnp.where(
            column == 0, one, jnp.where(column == 1, two, jnp.where(column == 2, three, 0.0))
        ).astype(bf16)
        grads_full = jnp.where(mine, grads, extra)
        values_full = jnp.where(mine, values, three_ones)
        for start in range(0, SEQ_LEN, SPAN):
            here = slice(start, start + SPAN)
            later = slice(start + SPAN, SEQ_LEN)
            near = jnp.where(keep, dot_nt(keys_full[here], query_full[here]), FAR)
            near = jnp.exp(near)
            near_grad = (near * dot_nt(values_full[here], grads_full[here])).astype(bf16)
            value_grad = dot(near.astype(bf16), grads[here])
            key_grad = dot(near_grad, query[here])
            query_near = dot_tn(near_grad, keys[here])
            if start:
                hold_ref[here, :] += query_near
            else:
                hold_ref[here, :] = query_near
            if start + SPAN < SEQ_LEN:
                past = jnp.exp(dot_nt(keys_full[here], query_full[later]))
                past_grad = (past * dot_nt(values_full[here], grads_full[later])).astype(bf16)
                value_grad = value_grad + dot(past.astype(bf16), grads[later])
                key_grad = key_grad + dot(past_grad, query[later])
                query_past = dot_tn(past_grad, keys[here])
                if start:
                    hold_ref[later, :] += query_past
                else:
                    hold_ref[later, :] = query_past
            key_grad = key_grad.astype(bf16)
            value_grad = value_grad.astype(bf16)
            if head:
                key_grad = jnp.where(upper_rows, key_grad, back_ref[here, LANES : 2 * LANES])
                value_grad = jnp.where(upper_rows, value_grad, back_ref[here, 2 * LANES :])
            back_ref[here, LANES : 2 * LANES] = key_grad
            back_ref[here, 2 * LANES :] = value_grad
        query_grad = (hold_ref[...] * (HDIM**-0.5)).astype(bf16)
        if head:
            query_grad = jnp.where(upper, query_grad, back_ref[:, :LANES])
        back_ref[:, :LANES] = query_grad


def attention_specs():
    return [
        pl.BlockSpec((SEQ_LEN, 3 * LANES), lambda s, h: (s, h)),
        pl.BlockSpec((1, SEQ_LEN, LANES), lambda s, h: (s, 0, 0)),
        pl.BlockSpec((1, SEQ_LEN, LANES), lambda s, h: (s, 0, 0)),
        pl.BlockSpec((2, 8, LANES), lambda s, h: (h, 0, 0)),
    ]


def pair_spec():
    return pl.BlockSpec((SEQ_LEN, LANES), lambda s, h: (s, h))


def attend_forward(qkv, columns):
    rows, width = qkv.shape
    pairs = width // (3 * LANES)
    seqs = rows // SEQ_LEN
    work = seqs * pairs * 2 * SEQ_LEN * SEQ_LEN
    return pl.pallas_call(
        forward_kernel,
        grid=(seqs, pairs),
        in_specs=attention_specs(),
        out_specs=[pair_spec(), pair_spec()],
        out_shape=[
            jax.ShapeDtypeStruct((rows, pairs * LANES), bf16),
            jax.ShapeDtypeStruct((rows, pairs * LANES), f32),
        ],
        compiler_params=pltpu.CompilerParams(vmem_limit_bytes=40 * 1024 * 1024),
        cost_estimate=pl.CostEstimate(
            flops=work * 320, bytes_accessed=rows * width * 4, transcendentals=work * 5 // 8
        ),
    )(qkv, *columns)


def attend_backward(qkv, columns, context, totals, grads):
    rows, width = qkv.shape
    pairs = width // (3 * LANES)
    seqs = rows // SEQ_LEN
    work = seqs * pairs * 2 * SEQ_LEN * SEQ_LEN
    return pl.pallas_call(
        backward_kernel,
        grid=(seqs, pairs),
        in_specs=attention_specs() + [pair_spec(), pair_spec(), pair_spec()],
        out_specs=pl.BlockSpec((SEQ_LEN, 3 * LANES), lambda s, h: (s, h)),
        out_shape=jax.ShapeDtypeStruct((rows, width), bf16),
        scratch_shapes=[pltpu.VMEM((SEQ_LEN, LANES), f32)],
        compiler_params=pltpu.CompilerParams(vmem_limit_bytes=40 * 1024 * 1024),
        cost_estimate=pl.CostEstimate(
            flops=work * 800, bytes_accessed=rows * width * 8, transcendentals=work * 5 // 8
        ),
    )(qkv, *columns, context, totals, grads)


def interleave(query, key, value):
    rows, width = query.shape
    parts = [part.reshape(rows, width // LANES, LANES) for part in (query, key, value)]
    return jnp.stack(parts, 2).reshape(rows, 3 * width)


def separate(joined):
    rows, width = joined.shape
    parts = joined.reshape(rows, width // (3 * LANES), 3, LANES)
    return [parts[:, :, which].reshape(rows, width // 3) for which in range(3)]


def shards(
    tokens,
    doc_lengths,
    ln1_gain,
    ln1_bias,
    w_query,
    b_query,
    w_key,
    w_value,
    b_value,
    w_dense,
    b_dense,
    ln2_gain,
    ln2_bias,
    w_up,
    b_up,
    w_down,
    b_down,
    out_grad,
):
    own_rows = tokens.shape[0]
    groups = lax.axis_size("tensor")
    group = lax.axis_index("tensor")
    alone = own_rows % SEQ_LEN == 0
    parts = groups if alone else 1
    axes = ("tensor", "dp") if alone else "dp"
    if alone:
        seqs = own_rows // SEQ_LEN
        doc_lengths = lax.dynamic_slice_in_dim(doc_lengths, group * seqs, seqs)

    def gathered(shard):
        full = lax.all_gather(shard, axes, axis=0, tiled=True)
        full = full.reshape((parts, full.shape[0] // parts, full.shape[1]))
        return [full[part] for part in range(parts)]

    def scattered(pieces):
        stacked = jnp.concatenate([piece.astype(bf16) for piece in pieces], 0)
        return lax.psum_scatter(stacked, axes, scatter_dimension=0, tiled=True).astype(f32)

    def spread(rows):
        return rows if alone else lax.all_gather(rows, "tensor", axis=0, tiled=True)

    def collect(rows):
        if alone:
            return rows
        return lax.psum_scatter(
            rows.astype(bf16), "tensor", scatter_dimension=0, tiled=True
        ).astype(f32)

    def total_of(pieces):
        result = pieces[0]
        for piece in pieces[1:]:
            result = result + piece
        return result

    width = w_query.shape[1]
    local_heads = width // HDIM
    qkv_bias = interleave(b_query[None], jnp.zeros_like(b_query)[None], b_value[None])
    biases = jnp.concatenate([qkv_bias, b_up[None]], -1)
    if alone:
        biases = lax.all_gather(biases, "tensor", axis=0, tiled=True)
    biases = biases.astype(f32)

    qkv_w = gathered(interleave(w_query, w_key, w_value))
    dense_w = gathered(w_dense.T)
    up_w = gathered(w_up)
    down_w = gathered(w_down.T)

    columns = []
    for part in range(parts):
        first_head = (part if alone else group) * local_heads
        head_number = first_head + jnp.arange(local_heads, dtype=jnp.int32) + 1
        slopes = 2.0 ** (-8.0 * head_number.astype(f32) / HEADS)
        columns.append(place_columns(doc_lengths, slopes))

    field = tokens.astype(f32)
    gain_one = ln1_gain.astype(f32)
    gain_two = ln2_gain.astype(f32)
    out_one, normed_one, factor_one = normalize(field, gain_one, ln1_bias.astype(f32))
    norm_rows = spread(out_one.astype(bf16))
    grad_rows = spread(out_grad)
    every = range(parts)
    qkv = [
        (dot(norm_rows, qkv_w[part]) + biases[part, : 3 * width]).astype(bf16) for part in every
    ]
    context, totals = zip(*[attend_forward(qkv[part], columns[part]) for part in every])
    hidden_one = (
        field
        + collect(total_of([dot_nt(context[part], dense_w[part]) for part in every]))
        + b_dense.astype(f32)
    )
    out_two, normed_two, factor_two = normalize(hidden_one, gain_two, ln2_bias.astype(f32))
    mlp_rows = spread(out_two.astype(bf16))
    activated, slope_rows = [], []
    for part in every:
        up_field = dot(mlp_rows, up_w[part]) + biases[part, 3 * width :]
        gelu_field, gelu_pull = jax.vjp(gelu_tanh, up_field)
        activated.append(gelu_field.astype(bf16))
        slope_rows.append(gelu_pull(jnp.ones_like(up_field))[0].astype(bf16))
    branch_sum = collect(total_of([dot_nt(activated[part], down_w[part]) for part in every]))
    mixed = (hidden_one + branch_sum + b_down.astype(f32)).astype(bf16)

    up_grad = [
        (dot(grad_rows, down_w[part]) * slope_rows[part].astype(f32)).astype(bf16)
        for part in every
    ]
    down_w_sum = scattered([dot_tn(grad_rows, activated[part]) for part in every]).T
    up_w_sum = scattered([dot_tn(mlp_rows, up_grad[part]) for part in every])
    norm_two_grad = collect(total_of([dot_nt(up_grad[part], up_w[part]) for part in every]))
    outer_grad = out_grad.astype(f32)
    hidden_grad = outer_grad + norm_back(norm_two_grad, normed_two, factor_two, gain_two)
    branch_rows = spread(hidden_grad.astype(bf16))
    context_grad = [dot(branch_rows, dense_w[part]).astype(bf16) for part in every]
    dense_w_sum = scattered([dot_tn(branch_rows, context[part]) for part in every]).T
    qkv_grad = [
        attend_backward(qkv[part], columns[part], context[part], totals[part], context_grad[part])
        for part in every
    ]
    qkv_w_sum = scattered([dot_tn(norm_rows, qkv_grad[part]) for part in every])
    query_w_sum, key_w_sum, value_w_sum = separate(qkv_w_sum)
    norm_one_grad = collect(total_of([dot_nt(qkv_grad[part], qkv_w[part]) for part in every]))
    tokens_grad = (hidden_grad + norm_back(norm_one_grad, normed_one, factor_one, gain_one)).astype(
        bf16
    )
    bias_axes = ("dp", "tensor") if alone else "dp"
    up_b_sum = lax.psum(
        jnp.concatenate([jnp.sum(piece.astype(f32), 0) for piece in up_grad]), bias_axes
    )
    qkv_b_sum = lax.psum(
        jnp.concatenate([jnp.sum(piece.astype(f32), 0) for piece in qkv_grad]), bias_axes
    )
    if alone:
        up_b_sum = lax.dynamic_slice_in_dim(up_b_sum, group * b_up.shape[0], b_up.shape[0])
        qkv_b_sum = lax.dynamic_slice_in_dim(qkv_b_sum, group * 3 * width, 3 * width)
    query_b_sum, _, value_b_sum = [piece[0] for piece in separate(qkv_b_sum[None])]
    early = (
        jnp.sum(hidden_grad, 0),
        jnp.sum(norm_two_grad * normed_two, 0),
        jnp.sum(norm_two_grad, 0),
        jnp.sum(outer_grad, 0),
    )
    late = (jnp.sum(norm_one_grad * normed_one, 0), jnp.sum(norm_one_grad, 0))
    dense_b_sum, gain_two_sum, shift_two_sum, down_b_sum = lax.psum(early, ("dp", "tensor"))
    gain_one_sum, shift_one_sum = lax.psum(late, ("dp", "tensor"))
    return (
        mixed,
        tokens_grad,
        gain_one_sum,
        shift_one_sum,
        query_w_sum,
        query_b_sum,
        key_w_sum,
        value_w_sum,
        value_b_sum,
        dense_w_sum,
        dense_b_sum,
        gain_two_sum,
        shift_two_sum,
        up_w_sum,
        up_b_sum,
        down_w_sum,
        down_b_sum,
    )


def solution(mesh):
    placed = (
        P(("dp", "tensor"), None),
        P("dp", None),
        P(),
        P(),
        P("dp", "tensor"),
        P("tensor"),
        P("dp", "tensor"),
        P("dp", "tensor"),
        P("tensor"),
        P("tensor", "dp"),
        P(),
        P(),
        P(),
        P("dp", "tensor"),
        P("tensor"),
        P("tensor", "dp"),
        P(),
        P(("dp", "tensor"), None),
    )
    return jax.shard_map(
        shards,
        mesh=mesh,
        in_specs=placed,
        out_specs=(
            P(("dp", "tensor"), None),
            P(("dp", "tensor"), None),
            P(),
            P(),
            P("dp", "tensor"),
            P("tensor"),
            P("dp", "tensor"),
            P("dp", "tensor"),
            P("tensor"),
            P("tensor", "dp"),
            P(),
            P(),
            P(),
            P("dp", "tensor"),
            P("tensor"),
            P("tensor", "dp"),
            P(),
        ),
        check_vma=False,
    )
```
